32 devices in a mesh: groups: 1, context: 8 (over y, x, core), span: 4 (over z).
Axes of the slice: x: 2, y: 2, z: 4, core: 2. Of those that a mesh axis runs over, the one named last changes fastest.
Arguments:
- raw_tokens: bfloat16 [1536, 2048], P(('groups', 'context'), 'span'), may hold values from -6 to 6
- keep: int32 [8, 32], P(('groups', 'context')), may hold values from -1 to 191, as said below
- attn_gain: float32 [2048], replicated, may hold values from 0.25 to 1.75
- query_weight: bfloat16 [2048, 4608], P(None, 'span'), may hold values from -5 to 5
- latent_weight: bfloat16 [2048, 576], P(None, 'span'), may hold values from -0.5 to 0.5
- kv_gain: float32 [512], replicated, may hold values from 0.25 to 1.75
- out_weight: bfloat16 [4096, 2048], P('span', 'context'), may hold values from -0.25 to 0.25
- moe_gain: float32 [2048], replicated, may hold values from 0.25 to 1.75
- expert_ids: int32 [256, 6], P(('groups', 'context', 'span')), may hold values from 0 to 15, all different within a row; in each aligned block of 8 rows (0 to 7, 8 to 15, ...) at most 6 rows name the same one
- gate_values: float32 [256, 6], P(('groups', 'context', 'span')), may hold values from 0.05 to 0.5
- expert_slot: int32 [16], replicated, may hold values from 0 to 15, each once
- expert_in: bfloat16 [32, 2, 2048, 704], P(('context', 'span')), may hold values from -0.125 to 0.125
- expert_out: bfloat16 [32, 704, 2048], P(('context', 'span')), may hold values from -0.15625 to 0.15625
Outputs:
- layer_out: bfloat16 [256, 2048], P(('groups', 'context', 'span'))
- latent_cache: bfloat16 [256, 576], P(('groups', 'context'))
The draws below stay inside these ranges and needn't reach their ends.
Inputs may be any that keep to these rules, and one draw needn't show every extreme that they name: `keep`: row c lists the kept positions among the 192 raw tokens of span c in increasing order, then -1 in the empty entries; every span keeps 32 // 2 or more, and in every draw some span keeps 32. `expert_ids`: in each aligned block of 8 rows (the rows of one device) no expert is named more than 6 times, a bound that some block reaches. `expert_slot`: each stored slot holds exactly one routed expert.
All inputs are finite; a program needn't handle non-finite values.
Results may differ from the reference program's by a relative error of at most 0.013.
Values may be sent and summed in bfloat16 or wider, within the bound.
A program may use at most 64 MiB of HBM per device.

```python
import math
import jax
import jax.numpy as jnp
import numpy as np
from jax import lax

D = 2048
HEADS = 8
KV_RANK = 512
ROPE = 64
LATENT = 576
HID = 1408
HALF = 704
EXPERTS = 16
TOP = 6
ROWS_DEV = 8
KEEP_C = 32
RAW_C = 192
TOKENS = 256
CAP = 6
N_CONTEXT = 8


def latent_base(key):
    return jax.random.truncated_normal(jax.random.fold_in(key, 11), -4.0, 4.0, (D, LATENT), jnp.float32) / math.sqrt(D)


def draw_latent_weight(key, part):
    return latent_base(key).astype(jnp.bfloat16)


def draw_query_weight(key, part):
    drawn = jax.random.truncated_normal(jax.random.fold_in(key, 23), -4.0, 4.0, (D, HEADS, LATENT), jnp.float32) / math.sqrt(D)
    return drawn.reshape(D, HEADS * LATENT).astype(jnp.bfloat16)


def draw_keep(key, part):
    span_keys = jax.random.split(jax.random.fold_in(key, 3), N_CONTEXT)
    orders = jax.vmap(lambda sub: jax.random.permutation(sub, RAW_C))(span_keys)[:, :KEEP_C].astype(jnp.int32)
    counts = jax.random.randint(jax.random.fold_in(key, 5), (N_CONTEXT,), KEEP_C // 2, KEEP_C + 1).astype(jnp.int32)
    fullest = jax.random.randint(jax.random.fold_in(key, 7), (), 0, N_CONTEXT).astype(jnp.int32)
    counts = jnp.where(jnp.arange(N_CONTEXT, dtype=jnp.int32) == fullest, KEEP_C, counts)
    entry = jnp.arange(KEEP_C, dtype=jnp.int32)[None, :]
    chosen = jnp.where(entry < counts[:, None], orders, RAW_C)
    chosen = jnp.sort(chosen, axis=1)
    return jnp.where(chosen >= RAW_C, -1, chosen).astype(jnp.int32)


def steps_of(rng, dims, cuts, low, top_value):
    def one(position, shards_of):
        heights = jax.random.uniform(jax.random.fold_in(jax.random.fold_in(rng, 6), position), (shards_of,), jnp.float32, low / len(cuts), top_value / len(cuts))
        return jnp.repeat(jnp.exp(heights), dims[position] // shards_of).reshape((-1,) + (1,) * (len(dims) - position - 1))

    level = one(*cuts[0])
    for cut in cuts[1:]:
        level = level * one(*cut)
    return level


def routed_block(key, own, number, rows, count, top, limit, skew):
    ranking = jax.random.permutation(key, count)
    heavy_load, ordinary = portions_of(count, rows * top, limit, skew, True), portions_of(count, rows * top, limit, skew, False)
    places = jnp.arange(count)

    def named(lengths, offset_by):
        used = int((lengths > 0).sum())
        fixed = max(1, used // 4)
        passed = fixed + (places - fixed + offset_by * (used - fixed)) % max(1, count - fixed)
        return jnp.zeros((count,), jnp.int32).at[ranking[jnp.where(places < fixed, places, passed)]].set(jnp.asarray(lengths, jnp.int32))

    lengths = jnp.where(number % 4 == 0, named(heavy_load, number // 4), named(ordinary, number - number // 4 - 1))
    mixed = jax.random.permutation(jax.random.fold_in(own, 3), count)
    giver, sink = mixed[0:count // 2 * 2:2], mixed[1:count // 2 * 2:2]
    room = jnp.minimum(lengths[giver] - 1, limit - lengths[sink]) // 2
    room = jnp.where((giver == ranking[0]) | (sink == ranking[0]) | (lengths[sink] == 0), 0, jnp.maximum(room, 0))
    passed = jax.random.randint(jax.random.fold_in(own, 4), (count // 2,), 0, 1 << 20) % (room + 1)
    lengths = lengths.at[giver].add(-passed).at[sink].add(passed)
    members = jnp.searchsorted(jnp.cumsum(lengths), jnp.arange(rows * top), side="right").astype(jnp.int32)
    listing = members.reshape(top, rows).T
    listing = listing[jax.random.permutation(jax.random.fold_in(own, 1), rows)]
    offset_by = jax.random.randint(jax.random.fold_in(own, 2), (rows, 1), 0, top)
    return jnp.take_along_axis(listing, (jnp.arange(top)[None, :] + offset_by) % top, axis=1)


def portions_of(number_of, total, limit, slope, full):
    portions = [(1 << 20) // math.isqrt(rank ** slope) + 1 for rank in range(1, number_of + 1)]
    largest = limit if full else min(limit, max(-(-total // number_of), total * portions[0] // sum(portions)))
    least = 1 if total - largest >= number_of - 1 else 0
    holding, spare = [largest] + [least] * (number_of - 1), total - largest - least * (number_of - 1)
    while spare > 0:
        candidates = [i for i in range(1, number_of) if holding[i] < largest] or [i for i in range(1, number_of) if holding[i] < limit]
        whole, budget = sum([portions[i] for i in candidates]), spare
        for i in candidates:
            addition = min(limit - holding[i], max(1, budget * portions[i] // whole), spare)
            holding[i] = holding[i] + addition
            spare = spare - addition
    return np.array(holding)


def bell_draw(own_key, extent, width, bound, cuts=(), kind=jnp.bfloat16):
    entries = width * jax.random.normal(own_key, extent, jnp.float32)
    if cuts:
        entries = entries * steps_of(own_key, extent, cuts, -0.22, 0.18)
    return jnp.clip(entries, -bound, bound).astype(kind)


def setup_inputs(seed: int = 0, part: int = 0) -> dict:
    arg_keys = jax.random.split(jax.random.key(seed), 14)
    own_keys = jax.random.split(jax.random.fold_in(arg_keys[13], part), 14)
    raw_tokens = bell_draw(own_keys[0], (N_CONTEXT * RAW_C, D), 1.0, 6.0, ((0, 8), (1, 4)))
    keep = draw_keep(jax.random.fold_in(jax.random.fold_in(arg_keys[13], part), 71), part)
    attn_gain = jnp.clip(1.0 + 0.15 * jax.random.normal(arg_keys[2], (D,), jnp.float32), 0.25, 1.75)
    query_weight = draw_query_weight(jax.random.fold_in(arg_keys[13], 71), part)
    latent_weight = draw_latent_weight(jax.random.fold_in(arg_keys[13], 71), part)
    kv_gain = jnp.clip(1.0 + 0.15 * jax.random.normal(arg_keys[5], (KV_RANK,), jnp.float32), 0.25, 1.75)
    out_weight = bell_draw(arg_keys[6], (HEADS * KV_RANK, D), KV_RANK ** -0.5, 0.25, ((0, 4), (1, 8)))
    moe_gain = jnp.clip(1.0 + 0.15 * jax.random.normal(arg_keys[7], (D,), jnp.float32), 0.25, 1.75)
    expert_ids_keys = jax.random.split(jax.random.fold_in(own_keys[8], 1), TOKENS // ROWS_DEV)
    expert_ids_turns = jax.random.permutation(jax.random.fold_in(own_keys[8], 3), TOKENS // ROWS_DEV)
    expert_ids = jax.vmap(lambda own, number: routed_block(jax.random.fold_in(own_keys[8], 2), own, number, ROWS_DEV, EXPERTS, TOP, CAP, 2))(expert_ids_keys, expert_ids_turns).reshape((TOKENS, TOP))
    gate_values = jnp.clip(jnp.exp(math.log(0.5) - 2.3025851 * jax.random.uniform(own_keys[9], (TOKENS, TOP), jnp.float32) ** steps_of(own_keys[9], (TOKENS, TOP), ((0, 32),), -0.2, 0.2)), 0.05, 0.5)
    expert_slot = jax.random.permutation(arg_keys[10], EXPERTS).astype(jnp.int32)
    expert_in = bell_draw(arg_keys[11], (2 * EXPERTS, 2, D, HALF), D ** -0.5, 0.125, ((0, 32),))
    expert_out = bell_draw(arg_keys[12], (2 * EXPERTS, HALF, D), HID ** -0.5, 0.15625, ((0, 32),))
    return dict(raw_tokens=raw_tokens, keep=keep, attn_gain=attn_gain, query_weight=query_weight, latent_weight=latent_weight, kv_gain=kv_gain, out_weight=out_weight, moe_gain=moe_gain, expert_ids=expert_ids, gate_values=gate_values, expert_slot=expert_slot, expert_in=expert_in, expert_out=expert_out)


EPS = 1e-06
THETA = 50000.0
SCALE = 192.0 ** (-0.5)

def rms_scale(values, gain):
    values = values.astype(jnp.float32)
    factor = lax.rsqrt(lax.optimization_barrier(jnp.mean(values * values, axis=-1, keepdims=True)) + EPS)
    return values * factor * gain.astype(jnp.float32)

def rotary_tables(positions, rotary_width):
    half = rotary_width // 2
    freqs = THETA ** (-2.0 * jnp.arange(half, dtype=jnp.float32) / rotary_width)
    angles = positions.astype(jnp.float32)[:, None] * freqs[None, :]
    return (jnp.cos(angles), jnp.sin(angles))

def rotate(values, cosine, sine):
    half = values.shape[-1] // 2
    first = values[..., :half]
    second = values[..., half:]
    return jnp.concatenate([first * cosine - second * sine, second * cosine + first * sine], axis=-1)

def reference(raw_tokens, keep, attn_gain, query_weight, latent_weight, kv_gain, out_weight, moe_gain, expert_ids, gate_values, expert_slot, expert_in, expert_out):
    slot_count = N_CONTEXT * KEEP_C
    span_ids = jnp.arange(N_CONTEXT, dtype=jnp.int32)[:, None]
    live = (keep >= 0).reshape(slot_count)
    positions = (span_ids * RAW_C + jnp.maximum(keep, 0)).reshape(slot_count).astype(jnp.int32)
    compact = jnp.take(raw_tokens, positions, axis=0)
    compact = jnp.where(live[:, None], compact, jnp.zeros_like(compact))
    normed = rms_scale(compact, attn_gain).astype(jnp.bfloat16)
    cosine, sine = rotary_tables(positions, ROPE)
    query = jnp.dot(normed, query_weight, preferred_element_type=jnp.float32).reshape(slot_count, HEADS, LATENT)
    query = jnp.concatenate([query[..., :KV_RANK], rotate(query[..., KV_RANK:], cosine[:, None, :], sine[:, None, :])], axis=-1).astype(jnp.bfloat16)
    latent = jnp.dot(normed, latent_weight, preferred_element_type=jnp.float32)
    latent_cache = jnp.concatenate([rms_scale(latent[:, :KV_RANK], kv_gain), rotate(latent[:, KV_RANK:], cosine, sine)], axis=-1).astype(jnp.bfloat16)
    order = jnp.arange(slot_count, dtype=jnp.int32)
    allowed = (order[None, :] <= order[:, None]) & live[None, :]
    values = latent_cache[:, :KV_RANK]

    def one_head(head_query):
        scores = jnp.dot(head_query, latent_cache.T, preferred_element_type=jnp.float32) * SCALE
        scores = jnp.where(allowed, scores, -jnp.inf)
        highest = lax.optimization_barrier(jnp.max(scores, axis=1, keepdims=True))
        weights = jnp.where(allowed, jnp.exp(scores - highest), 0.0)
        denominator = lax.optimization_barrier(jnp.sum(weights, axis=1, keepdims=True))
        summed = jnp.dot(weights.astype(jnp.bfloat16), values, preferred_element_type=jnp.float32)
        return (summed / denominator).astype(jnp.bfloat16)
    mixed = lax.map(one_head, jnp.swapaxes(query, 0, 1))
    heads_out = jnp.einsum('hqd,hdm->qm', mixed.astype(jnp.float32), out_weight.reshape(HEADS, KV_RANK, D).astype(jnp.float32))
    resid = compact.astype(jnp.float32) + heads_out
    moe_in = rms_scale(resid, moe_gain).astype(jnp.bfloat16)
    blocks = slot_count // ROWS_DEV
    slots = jnp.take(expert_slot, expert_ids, axis=0).astype(jnp.int32).reshape(blocks, ROWS_DEV * TOP)
    member = (slots[:, :, None] == jnp.arange(EXPERTS, dtype=jnp.int32)[None, None, :]).astype(jnp.int32)
    place = lax.optimization_barrier(jnp.sum((jnp.cumsum(member, axis=1) - member) * member, axis=2))
    target = (slots * CAP + place).reshape(blocks, ROWS_DEV, TOP)
    block_rows = moe_in.reshape(blocks, ROWS_DEV, D).astype(jnp.float32)
    gates = gate_values.reshape(blocks, ROWS_DEV, TOP).astype(jnp.float32)
    pieces_in = expert_in.reshape(EXPERTS, 2, 2, D, HALF)
    pieces_out = expert_out.reshape(EXPERTS, 2, HALF, D)
    capacity_ids = jnp.arange(CAP, dtype=jnp.int32)

    def one_expert(routed, operands):
        stored, weights_in, weights_out = operands
        hits = target[:, :, :, None] == (stored * CAP + capacity_ids)[None, None, None, :]
        select = lax.optimization_barrier(jnp.sum(hits.astype(jnp.float32), axis=2))
        buffer = jnp.einsum('brc,brd->bcd', select, block_rows, precision=lax.Precision.HIGHEST).astype(jnp.bfloat16).reshape(blocks * CAP, D)
        result = jnp.zeros((blocks * CAP, D), jnp.float32)
        for half in range(2):
            gate = jnp.dot(buffer, weights_in[half, 0], preferred_element_type=jnp.float32)
            upper = jnp.dot(buffer, weights_in[half, 1], preferred_element_type=jnp.float32)
            hidden = (jax.nn.silu(gate) * upper).astype(jnp.bfloat16)
            part = jnp.dot(hidden, weights_out[half], preferred_element_type=jnp.float32).astype(jnp.bfloat16)
            result = result + part.astype(jnp.float32)
        result = result.reshape(blocks, CAP, D)
        combine = lax.optimization_barrier(jnp.sum(jnp.where(hits, gates[:, :, :, None], 0.0), axis=2))
        routed = routed + jnp.einsum('brc,bcd->brd', combine, result, precision=lax.Precision.HIGHEST)
        return (routed, None)
    start = jnp.zeros((blocks, ROWS_DEV, D), jnp.float32)
    routed, _ = lax.scan(one_expert, start, (jnp.arange(EXPERTS, dtype=jnp.int32), pieces_in, pieces_out))
    routed = routed.reshape(slot_count, D)
    layer_out = jnp.where(live[:, None], resid + routed, 0.0).astype(jnp.bfloat16)
    return (layer_out, latent_cache)
```

```python
import functools

import jax
import jax.numpy as jnp
from jax import lax
from jax.experimental import pallas as pl
from jax.experimental.pallas import tpu as pltpu
from jax.sharding import PartitionSpec as P

EPS = 1e-06
THETA = 50000.0
SCALE = 192.0 ** (-0.5)
NEGATIVE = -1e30
F32 = jnp.float32
BF16 = jnp.bfloat16


def xor(value, bits):
    out = value
    bit = 1
    while bit <= bits:
        if bits & bit:
            out = out + bit * (1 - 2 * ((value // bit) % 2))
        bit *= 2
    return out


def rotate(values, cosine, sine):
    half = values.shape[-1] // 2
    swapped = jnp.concatenate([values[:, half:], values[:, :half]], axis=1)
    return values * cosine + swapped * sine


def normalized(values, gain):
    factor = lax.rsqrt(jnp.mean(values * values, axis=-1, keepdims=True) + EPS)
    return values * factor * gain


def dot(a, b):
    return jnp.dot(a, b, preferred_element_type=F32)


def kernel(
    n,
    spans,
    raw,
    keep,
    cosine,
    sine,
    attn_gain,
    kv_gain,
    moe_gain,
    ids,
    gate_values,
    slot_col,
    query_hbm,
    latent_hbm,
    out_hbm,
    in_hbm,
    down_hbm,
    layer_out,
    cache_out,
    query_w,
    latent_w,
    out_w,
    in_w,
    down_w,
    picked,
    normed,
    query_acc,
    latents,
    keys,
    mixed,
    part_send,
    part_recv,
    att_send,
    att_recv,
    folded,
    moe_rows,
    gate_acc,
    up_acc,
    pair_send,
    pair_recv,
    own_sum,
    plane_send,
    plane_recv,
    last_send,
    last_recv,
    load_sem,
    z_send,
    z_recv,
    p_send,
    p_recv,
    pair_sem,
):
    c = lax.axis_index("context")
    s = lax.axis_index("span")
    core = c % 2
    half_n = n // 2
    keep_count = keep.shape[0]
    rows_dev = layer_out.shape[0]
    model_width = layer_out.shape[1]
    latent_width = cache_out.shape[1]
    kv_rank = kv_gain.shape[1]
    heads = query_w.shape[1] // latent_width
    experts = slot_col.shape[0]
    raw_rows = raw.shape[0]

    def slot(ctx):
        return (ctx % 2) * half_n + ctx // 2

    sources = (query_hbm, latent_hbm, out_hbm, in_hbm, down_hbm)
    targets = (query_w, latent_w, out_w, in_w, down_w)
    loads = [
        pltpu.make_async_copy(a, b, load_sem.at[i])
        for i, (a, b) in enumerate(zip(sources, targets))
    ]
    for i in (1, 0, 2, 3, 4):
        loads[i].start()

    barrier = pltpu.get_barrier_semaphore()
    for k in range(1, n):
        pl.semaphore_signal(
            barrier, 1, device_id={"context": xor(c, k)}, device_id_type=pl.DeviceIdType.MESH
        )
    for k in range(1, spans):
        pl.semaphore_signal(
            barrier, 1, device_id={"span": xor(s, k)}, device_id_type=pl.DeviceIdType.MESH
        )

    def remote(src, dst, axis, peer, send, recv):
        return pltpu.make_async_remote_copy(
            src_ref=src,
            dst_ref=dst,
            send_sem=send,
            recv_sem=recv,
            device_id={axis: peer},
            device_id_type=pl.DeviceIdType.MESH,
        )

    pending = []

    def push(*args):
        copy = remote(*args)
        copy.start()
        pending.append(copy)

    def z_gather_start(buf, phase):
        for k in range(1, spans):
            push(
                buf.at[s], buf.at[s], "span", xor(s, k), z_send.at[phase, k], z_recv.at[phase, k]
            )

    def z_gather_wait(buf, phase):
        for k in range(1, spans):
            peer = xor(s, k)
            remote(
                buf.at[s], buf.at[peer], "span", peer, z_send.at[phase, k], z_recv.at[phase, k]
            ).wait_recv()

    def z_scatter(send_buf, recv_buf, phase):
        for k in range(1, spans):
            peer = xor(s, k)
            push(
                send_buf.at[peer],
                recv_buf.at[s],
                "span",
                peer,
                z_send.at[phase, k],
                z_recv.at[phase, k],
            )

    def z_scatter_sum(send_buf, recv_buf, phase):
        total = send_buf[s].astype(F32)
        for k in range(1, spans):
            peer = xor(s, k)
            remote(
                send_buf.at[peer],
                recv_buf.at[peer],
                "span",
                peer,
                z_send.at[phase, k],
                z_recv.at[phase, k],
            ).wait_recv()
            total = total + recv_buf[peer].astype(F32)
        return total

    def p_block(buf, phase, k, peer, block):
        return (
            buf.at[slot(block)],
            buf.at[slot(block)],
            "context",
            peer,
            p_send.at[phase, k],
            p_recv.at[phase, k],
        )

    def p_gather_start(buf, phase):
        for k in range(n - 1, 0, -2):
            push(*p_block(buf, phase, k, xor(c, k), c))

    def p_gather_forward(buf, phase):
        for k in range(1, n, 2):
            block = xor(c, k)
            remote(*p_block(buf, phase, k, block, block)).wait_recv()
            if k > 1:
                push(*p_block(buf, phase, k - 1, xor(c, 1), block))

    def p_gather_finish(buf, phase):
        for k in range(2, n, 2):
            block = xor(c, k)
            remote(*p_block(buf, phase, k, block, block)).wait_recv()

    listing = keep[...]
    live = listing >= 0
    chosen = lax.broadcasted_iota(jnp.int32, (keep_count, raw_rows), 1) == listing
    picked[s] = dot(chosen.astype(F32).astype(BF16), raw[...]).astype(BF16)

    pl.semaphore_wait(barrier, n - 1 + spans - 1)
    z_gather_start(picked, 0)
    hits = jnp.zeros((rows_dev, experts), F32)
    expert_lane = lax.broadcasted_iota(jnp.int32, (rows_dev, experts), 1)
    for t in range(ids.shape[1]):
        hits = hits + jnp.where(ids[:, t : t + 1] == expert_lane, gate_values[:, t : t + 1], 0.0)
    hits_high = hits.astype(BF16)
    hits_low = (hits - hits_high.astype(F32)).astype(BF16)
    lane = lax.broadcasted_iota(jnp.int32, (experts, 128), 1)
    place_high = (lane == slot_col[...]).astype(F32).astype(BF16)
    place_low = (lane == slot_col[...] + 64).astype(F32).astype(BF16)
    gate_lanes = dot(hits_high, place_high) + dot(hits_low, place_low)
    z_gather_wait(picked, 0)
    compact = jnp.concatenate([picked[i] for i in range(spans)], axis=1).astype(F32)
    normed[...] = normalized(compact, attn_gain[...]).astype(BF16)
    own_rows = jnp.zeros((rows_dev, model_width), F32)
    own_keep = jnp.zeros((rows_dev, 1), jnp.int32)
    for i in range(spans):
        own_rows = jnp.where(s == i, compact[i * rows_dev : (i + 1) * rows_dev], own_rows)
        own_keep = jnp.where(s == i, listing[i * rows_dev : (i + 1) * rows_dev], own_keep)

    loads[1].wait()
    latents[s] = dot(normed[...], latent_w[...])
    z_gather_start(latents, 1)
    loads[0].wait()
    query_acc[...] = jnp.zeros_like(query_acc)
    depth = 512

    def query_step(i, _):
        cut = pl.ds(pl.multiple_of(i * depth, depth), depth)
        query_acc[...] += dot(normed[:, cut], query_w[cut, :])
        return 0

    lax.fori_loop(0, model_width // depth, query_step, 0)
    z_gather_wait(latents, 1)
    latent = jnp.concatenate([latents[i] for i in range(spans)], axis=1)
    cos2, sin2 = cosine[...], sine[...]
    pad = -latent_width % 128
    flags = jnp.where(
        (lax.broadcasted_iota(jnp.int32, (keep_count, pad), 1) == 0) & live, 1.0, 0.0
    )
    tail = jnp.concatenate([rotate(latent[:, kv_rank:], cos2, sin2), flags], axis=1)
    block = jnp.concatenate([normalized(latent[:, :kv_rank], kv_gain[...]), tail], axis=1)
    block = block.astype(BF16)
    keys[slot(c)] = block
    p_gather_start(keys, 0)
    cache_out[...] = block[:, :latent_width]
    parts = []
    for h in range(heads):
        q = query_acc[:, h * latent_width : (h + 1) * latent_width]
        parts.append(
            jnp.concatenate(
                [
                    q[:, :kv_rank],
                    rotate(q[:, kv_rank:], cos2, sin2),
                    jnp.zeros((keep_count, pad), F32),
                ],
                axis=1,
            )
        )
    query = jnp.concatenate(parts, axis=0).astype(BF16)
    tokens = n * keep_count
    rows = heads * keep_count
    key_lane = lax.broadcasted_iota(jnp.int32, (rows, tokens), 1)
    query_row = lax.broadcasted_iota(jnp.int32, (rows, tokens), 0) & (keep_count - 1)
    shift = keep_count.bit_length() - 1
    key_slot = lax.shift_right_logical(key_lane, shift)
    key_ctx = (key_slot & (half_n - 1)) * 2 + lax.shift_right_logical(
        key_slot, half_n.bit_length() - 1
    )
    causal = key_ctx * keep_count + (key_lane & (keep_count - 1)) <= query_row + c * keep_count
    pick_flag = jnp.where(
        lax.broadcasted_iota(jnp.int32, (16, latent_width + pad), 1) == latent_width, 1.0, 0.0
    ).astype(BF16)
    p_gather_forward(keys, 0)
    p_gather_finish(keys, 0)
    all_keys = keys[...].reshape(tokens, latent_width + pad)
    contract = (((1,), (1,)), ((), ()))
    scores = lax.dot_general(query, all_keys, contract, preferred_element_type=F32) * SCALE
    key_live = lax.dot_general(pick_flag, all_keys, contract, preferred_element_type=F32)[:1]
    allowed = causal & (key_live > 0)
    scores = jnp.where(allowed, scores, NEGATIVE)
    highest = jnp.max(scores, axis=1, keepdims=True)
    weights = jnp.where(allowed, jnp.exp(scores - highest), 0.0)
    denominator = jnp.sum(weights, axis=1, keepdims=True)
    summed = dot(weights.astype(BF16), all_keys[:, :kv_rank]) / denominator
    mixed[slot(c)] = jnp.concatenate(
        [summed[h * keep_count : (h + 1) * keep_count] for h in range(heads)], axis=1
    ).astype(BF16)
    p_gather_start(mixed, 1)
    loads[2].wait()
    p_gather_forward(mixed, 1)
    p_gather_finish(mixed, 1)
    columns = out_w.shape[1]
    projected = dot(mixed[...].reshape(tokens, heads * kv_rank), out_w[...])
    projected = projected.reshape(n, spans, rows_dev, columns)
    for i in range(spans):
        part_send[i] = projected[:, i].reshape(n * rows_dev, columns).astype(BF16)
    z_scatter(part_send, part_recv, 2)
    attended = z_scatter_sum(part_send, part_recv, 2)
    for i in range(n):
        att_send[i] = attended[i * rows_dev : (i + 1) * rows_dev]
    for k in range(n - 1, 0, -1):
        peer = xor(c, k)
        push(
            att_send.at[slot(peer)],
            att_recv.at[c],
            "context",
            peer,
            p_send.at[2, k],
            p_recv.at[2, k],
        )
    att_recv[c] = att_send[slot(c)]
    for k in range(1, n):
        peer = xor(c, k)
        remote(
            att_send.at[slot(peer)],
            att_recv.at[peer],
            "context",
            peer,
            p_send.at[2, k],
            p_recv.at[2, k],
        ).wait_recv()
    resid = own_rows + jnp.concatenate([att_recv[i] for i in range(n)], axis=1)
    moe_in = normalized(resid, moe_gain[...])
    half_width = folded.shape[2]
    wide = jnp.concatenate(
        [moe_in, gate_lanes, jnp.zeros((rows_dev, 2 * half_width - model_width - 128), F32)],
        axis=1,
    )
    folded[s] = jnp.concatenate([wide[:, :half_width], wide[:, half_width:]], axis=0).astype(BF16)
    z_gather_start(folded, 3)
    z_gather_wait(folded, 3)
    blocks = []
    for i in range(spans):
        v = folded[i].astype(F32)
        blocks.append(
            jnp.concatenate([v[:rows_dev], v[rows_dev:]], axis=1)[:, : model_width + 128]
        )
    moe_rows[slot(c)] = jnp.concatenate(blocks, axis=0).astype(BF16)
    p_gather_start(moe_rows, 3)

    stored = (c * spans + s) // 2
    many = half_n * keep_count
    width = 512

    def expert(base, target):
        lanes = lax.broadcasted_iota(jnp.int32, (many, 128), 1)
        gate_block = moe_rows[pl.ds(base, half_n), :, model_width:].reshape(many, 128)
        scale = jnp.sum(
            jnp.where(
                (lanes == stored) | (lanes == stored + 64), gate_block.astype(F32), 0.0
            ),
            axis=1,
            keepdims=True,
        )
        gate_acc[...] = jnp.zeros_like(gate_acc)
        up_acc[...] = jnp.zeros_like(up_acc)

        def step(i, _):
            cut = pl.ds(pl.multiple_of(i * depth, depth), depth)
            x = moe_rows[pl.ds(base, half_n), :, cut].reshape(many, depth)
            gate_acc[...] += dot(x, in_w[0, 0, cut, :])
            up_acc[...] += dot(x, in_w[0, 1, cut, :])
            return 0

        lax.fori_loop(0, model_width // depth, step, 0)
        gate = gate_acc[...]
        hidden = (gate / (1.0 + jnp.exp(-gate)) * up_acc[...]).astype(BF16)

        def down(i, _):
            cut = pl.ds(pl.multiple_of(i * width, width), width)
            made = dot(hidden, down_w[0, :, cut]) * scale
            target[:, :, cut] = made.reshape(half_n, keep_count, width).astype(BF16)
            return 0

        lax.fori_loop(0, model_width // width, down, 0)

    p_gather_forward(moe_rows, 3)
    loads[3].wait()
    loads[4].wait()
    expert((1 - core) * half_n, pair_send)
    pair = (pair_send, pair_recv, "context", xor(c, 1), pair_sem.at[0], pair_sem.at[1])
    push(*pair)
    p_gather_finish(moe_rows, 3)
    expert(core * half_n, own_sum)
    remote(*pair).wait_recv()
    for k in range(n - 2, 0, -2):
        peer = xor(c, k)
        chip = peer // 2
        plane_send[chip] = (own_sum[chip].astype(F32) + pair_recv[chip].astype(F32)).astype(BF16)
        push(
            plane_send.at[chip],
            plane_recv.at[c // 2],
            "context",
            peer,
            p_send.at[4, k],
            p_recv.at[4, k],
        )
    total = own_sum[c // 2].astype(F32) + pair_recv[c // 2].astype(F32)
    for k in range(2, n, 2):
        peer = xor(c, k)
        chip = peer // 2
        remote(
            plane_send.at[chip],
            plane_recv.at[chip],
            "context",
            peer,
            p_send.at[4, k],
            p_recv.at[4, k],
        ).wait_recv()
        total = total + plane_recv[chip].astype(F32)
    middle = model_width // 2
    for i in range(spans):
        v = total[i * rows_dev : (i + 1) * rows_dev]
        last_send[i] = jnp.concatenate([v[:, :middle], v[:, middle:]], axis=0).astype(BF16)
    z_scatter(last_send, last_recv, 4)
    routed = z_scatter_sum(last_send, last_recv, 4)
    routed = jnp.concatenate([routed[:rows_dev], routed[rows_dev:]], axis=1)
    layer_out[...] = jnp.where(own_keep >= 0, resid + routed, 0.0).astype(BF16)
    for copy in pending:
        copy.wait_send()


def per_device(
    raw_tokens,
    keep,
    attn_gain,
    query_weight,
    latent_weight,
    kv_gain,
    out_weight,
    moe_gain,
    expert_ids,
    gate_values,
    expert_slot,
    expert_in,
    expert_out,
):
    n = lax.axis_size("context")
    spans = lax.axis_size("span")
    kv_rank = kv_gain.shape[0]
    local_latent = latent_weight.shape[1]
    latent_width = local_latent * spans
    model_width = attn_gain.shape[0]
    keep_count = keep.shape[1]
    raw_rows = raw_tokens.shape[0]
    rows_dev = expert_ids.shape[0]
    rotary_width = latent_width - kv_rank
    half = rotary_width // 2
    key_width = latent_width + (-latent_width % 128)
    many = n // 2 * keep_count
    hidden = expert_in.shape[3]
    columns = out_weight.shape[1]
    mixed_width = out_weight.shape[0]
    wide = model_width + 128
    half_width = (wide + 255) // 256 * 128
    listing = keep[0]
    positions = lax.axis_index("context") * raw_rows + jnp.maximum(listing, 0)
    freqs = THETA ** (-2.0 * jnp.arange(half, dtype=F32) / rotary_width)
    angles = positions.astype(F32)[:, None] * freqs[None, :]
    cosine, sine = jnp.cos(angles), jnp.sin(angles)
    cos2 = jnp.concatenate([cosine, cosine], axis=1)
    sin2 = jnp.concatenate([-sine, sine], axis=1)
    vmem = pl.BlockSpec(memory_space=pltpu.VMEM)
    hbm = pl.BlockSpec(memory_space=pl.ANY)
    chips = n // 2
    return pl.pallas_call(
        functools.partial(kernel, n, spans),
        out_shape=(
            jax.ShapeDtypeStruct((rows_dev, model_width), BF16),
            jax.ShapeDtypeStruct((keep_count, latent_width), BF16),
        ),
        in_specs=[vmem] * 10 + [hbm] * 5,
        out_specs=(vmem, vmem),
        scratch_shapes=[
            pltpu.VMEM(query_weight.shape, BF16),
            pltpu.VMEM(latent_weight.shape, BF16),
            pltpu.VMEM(out_weight.shape, BF16),
            pltpu.VMEM(expert_in.shape, BF16),
            pltpu.VMEM(expert_out.shape, BF16),
            pltpu.VMEM((spans, keep_count, raw_tokens.shape[1]), BF16),
            pltpu.VMEM((keep_count, model_width), BF16),
            pltpu.VMEM((keep_count, query_weight.shape[1]), F32),
            pltpu.VMEM((spans, keep_count, local_latent), F32),
            pltpu.VMEM((n, keep_count, key_width), BF16),
            pltpu.VMEM((n, keep_count, mixed_width), BF16),
            pltpu.VMEM((spans, n * rows_dev, columns), BF16),
            pltpu.VMEM((spans, n * rows_dev, columns), BF16),
            pltpu.VMEM((n, rows_dev, columns), F32),
            pltpu.VMEM((n, rows_dev, columns), F32),
            pltpu.VMEM((spans, 2 * rows_dev, half_width), BF16),
            pltpu.VMEM((n, keep_count, wide), BF16),
            pltpu.VMEM((many, hidden), F32),
            pltpu.VMEM((many, hidden), F32),
            pltpu.VMEM((chips, keep_count, model_width), BF16),
            pltpu.VMEM((chips, keep_count, model_width), BF16),
            pltpu.VMEM((chips, keep_count, model_width), BF16),
            pltpu.VMEM((chips, keep_count, model_width), BF16),
            pltpu.VMEM((chips, keep_count, model_width), BF16),
            pltpu.VMEM((spans, 2 * rows_dev, model_width // 2), BF16),
            pltpu.VMEM((spans, 2 * rows_dev, model_width // 2), BF16),
            pltpu.SemaphoreType.DMA((5,)),
            pltpu.SemaphoreType.DMA((5, spans)),
            pltpu.SemaphoreType.DMA((5, spans)),
            pltpu.SemaphoreType.DMA((5, n)),
            pltpu.SemaphoreType.DMA((5, n)),
            pltpu.SemaphoreType.DMA((2,)),
        ],
        compiler_params=pltpu.CompilerParams(
            collective_id=0, has_side_effects=True, vmem_limit_bytes=56 * 1024 * 1024
        ),
    )(
        raw_tokens,
        listing[:, None],
        cos2,
        sin2,
        attn_gain[None, :],
        kv_gain[None, :],
        moe_gain[None, :],
        expert_ids,
        gate_values,
        expert_slot[:, None],
        query_weight,
        latent_weight,
        out_weight,
        expert_in,
        expert_out,
    )


def solution(mesh):
    placed = (
        P(("groups", "context"), "span"),
        P(("groups", "context"), None),
        P(),
        P(None, "span"),
        P(None, "span"),
        P(),
        P("span", "context"),
        P(),
        P(("groups", "context", "span"), None),
        P(("groups", "context", "span"), None),
        P(),
        P(("context", "span"), None, None, None),
        P(("context", "span"), None, None),
    )
    return jax.shard_map(
        per_device,
        mesh=mesh,
        in_specs=placed,
        out_specs=(P(("groups", "context", "span"), None), P(("groups", "context"), None)),
        check_vma=False,
    )
```

```python
import functools

import jax
import jax.numpy as jnp
import numpy as np
from jax import lax
from jax.experimental import pallas as pl
from jax.experimental.pallas import tpu as pltpu
from jax.sharding import PartitionSpec as P

EPS = 1e-06
THETA = 50000.0
SCALE = 192.0 ** (-0.5)
NEGATIVE = -1e30
F32 = jnp.float32
BF16 = jnp.bfloat16


def xor(value, bits):
    out = value
    bit = 1
    while bit <= bits:
        if bits & bit:
            out = out + bit * (1 - 2 * ((value // bit) % 2))
        bit *= 2
    return out


def rotate(values, cosine, sine):
    half = values.shape[-1] // 2
    swapped = jnp.concatenate([values[:, half:], values[:, :half]], axis=1)
    return values * cosine + swapped * sine


def normalized(values, gain):
    factor = lax.rsqrt(jnp.mean(values * values, axis=-1, keepdims=True) + EPS)
    return values * factor * gain


def dot(a, b):
    return jnp.dot(a, b, preferred_element_type=F32)


def dot_rows(a, b):
    return lax.dot_general(a, b, (((1,), (1,)), ((), ())), preferred_element_type=F32)


def column(row):
    size = row.shape[1]
    same = lax.broadcasted_iota(jnp.int32, (size, size), 0) == lax.broadcasted_iota(
        jnp.int32, (size, size), 1
    )
    return jnp.sum(jnp.where(same, row.astype(F32), 0.0), axis=1, keepdims=True).astype(jnp.int32)


def kernel(
    n,
    spans,
    raw,
    keep,
    freqs,
    attn_gain,
    kv_gain,
    moe_gain,
    ids,
    gate_values,
    slots,
    query_hbm,
    latent_hbm,
    out_hbm,
    in_hbm,
    down_hbm,
    layer_out,
    cache_out,
    query_w,
    latent_w,
    out_w,
    in_w,
    down_w,
    picked,
    normed,
    query_acc,
    latents,
    keys,
    mixed,
    part_send,
    part_recv,
    att_send,
    att_recv,
    folded,
    moe_rows,
    gate_acc,
    up_acc,
    pair_send,
    pair_recv,
    own_sum,
    plane_send,
    plane_recv,
    last_send,
    last_recv,
    load_sem,
    z_send,
    z_recv,
    p_send,
    p_recv,
    pair_sem,
):
    c = lax.axis_index("context")
    s = lax.axis_index("span")
    core = c % 2
    half_n = n // 2
    keep_count = keep.shape[1]
    rows_dev = layer_out.shape[0]
    model_width = layer_out.shape[1]
    latent_width = cache_out.shape[1]
    kv_rank = kv_gain.shape[1]
    heads = query_w.shape[1] // latent_width
    experts = slots.shape[1]
    raw_rows = raw.shape[0]

    def slot(ctx):
        return (ctx % 2) * half_n + ctx // 2

    sources = (query_hbm, latent_hbm, out_hbm, in_hbm, down_hbm)
    targets = (query_w, latent_w, out_w, in_w, down_w)
    loads = [
        pltpu.make_async_copy(a, b, load_sem.at[i])
        for i, (a, b) in enumerate(zip(sources, targets))
    ]
    for i in (1, 0, 2, 3, 4):
        loads[i].start()

    barrier = pltpu.get_barrier_semaphore()
    for k in range(1, n):
        pl.semaphore_signal(
            barrier, 1, device_id={"context": xor(c, k)}, device_id_type=pl.DeviceIdType.MESH
        )
    for k in range(1, spans):
        pl.semaphore_signal(
            barrier, 1, device_id={"span": xor(s, k)}, device_id_type=pl.DeviceIdType.MESH
        )

    def remote(src, dst, axis, peer, send, recv):
        return pltpu.make_async_remote_copy(
            src_ref=src,
            dst_ref=dst,
            send_sem=send,
            recv_sem=recv,
            device_id={axis: peer},
            device_id_type=pl.DeviceIdType.MESH,
        )

    pending = []

    def push(*args):
        copy = remote(*args)
        copy.start()
        pending.append(copy)

    def z_gather_start(buf, phase):
        for k in range(1, spans):
            push(
                buf.at[s], buf.at[s], "span", xor(s, k), z_send.at[phase, k], z_recv.at[phase, k]
            )

    def z_gather_wait(buf, phase):
        for k in range(1, spans):
            peer = xor(s, k)
            remote(
                buf.at[s], buf.at[peer], "span", peer, z_send.at[phase, k], z_recv.at[phase, k]
            ).wait_recv()

    def z_scatter(send_buf, recv_buf, phase):
        for k in range(1, spans):
            peer = xor(s, k)
            push(
                send_buf.at[peer],
                recv_buf.at[s],
                "span",
                peer,
                z_send.at[phase, k],
                z_recv.at[phase, k],
            )

    def z_scatter_sum(send_buf, recv_buf, phase):
        total = send_buf[s].astype(F32)
        for k in range(1, spans):
            peer = xor(s, k)
            remote(
                send_buf.at[peer],
                recv_buf.at[peer],
                "span",
                peer,
                z_send.at[phase, k],
                z_recv.at[phase, k],
            ).wait_recv()
            total = total + recv_buf[peer].astype(F32)
        return total

    def p_block(buf, phase, k, peer, block):
        return (
            buf.at[slot(block)],
            buf.at[slot(block)],
            "context",
            peer,
            p_send.at[phase, k],
            p_recv.at[phase, k],
        )

    def p_gather_start(buf, phase):
        for k in range(n - 1, 0, -2):
            push(*p_block(buf, phase, k, xor(c, k), c))

    def p_gather_forward(buf, phase):
        for k in range(1, n, 2):
            block = xor(c, k)
            remote(*p_block(buf, phase, k, block, block)).wait_recv()
            if k > 1:
                push(*p_block(buf, phase, k - 1, xor(c, 1), block))

    def p_gather_finish(buf, phase):
        for k in range(2, n, 2):
            block = xor(c, k)
            remote(*p_block(buf, phase, k, block, block)).wait_recv()

    listing = column(keep[...])
    live = listing >= 0
    chosen = lax.broadcasted_iota(jnp.int32, (keep_count, raw_rows), 1) == listing
    picked[s] = dot(chosen.astype(F32).astype(BF16), raw[...]).astype(BF16)

    pl.semaphore_wait(barrier, n - 1 + spans - 1)
    z_gather_start(picked, 0)
    hits = jnp.zeros((rows_dev, experts), F32)
    expert_lane = lax.broadcasted_iota(jnp.int32, (rows_dev, experts), 1)
    for t in range(ids.shape[1]):
        hits = hits + jnp.where(ids[:, t : t + 1] == expert_lane, gate_values[:, t : t + 1], 0.0)
    hits_high = hits.astype(BF16)
    hits_low = (hits - hits_high.astype(F32)).astype(BF16)
    lane = lax.broadcasted_iota(jnp.int32, (experts, 128), 1)
    slot_col = column(slots[...])
    place_high = (lane == slot_col).astype(F32).astype(BF16)
    place_low = (lane == slot_col + 64).astype(F32).astype(BF16)
    gate_lanes = dot(hits_high, place_high) + dot(hits_low, place_low)
    positions = (c * raw_rows + jnp.maximum(listing, 0)).astype(F32)
    angles = positions * freqs[...]
    cos2 = jnp.cos(angles)
    rotary = freqs.shape[1]
    first = lax.broadcasted_iota(jnp.int32, (keep_count, rotary), 1) < rotary // 2
    sin2 = jnp.where(first, -1.0, 1.0) * jnp.sin(angles)
    z_gather_wait(picked, 0)
    compact = jnp.concatenate([picked[i] for i in range(spans)], axis=1).astype(F32)
    normed[...] = normalized(compact, attn_gain[...]).astype(BF16)
    own_rows = jnp.zeros((rows_dev, model_width), F32)
    own_keep = jnp.zeros((rows_dev, 1), jnp.int32)
    for i in range(spans):
        own_rows = jnp.where(s == i, compact[i * rows_dev : (i + 1) * rows_dev], own_rows)
        own_keep = jnp.where(s == i, listing[i * rows_dev : (i + 1) * rows_dev], own_keep)

    loads[1].wait()
    latents[s] = dot_rows(normed[...], latent_w[...])
    z_gather_start(latents, 1)
    loads[0].wait()
    query_acc[...] = jnp.zeros_like(query_acc)
    depth = 512

    def query_step(i, _):
        cut = pl.ds(pl.multiple_of(i * depth, depth), depth)
        query_acc[...] += dot(normed[:, cut], query_w[cut, :])
        return 0

    lax.fori_loop(0, model_width // depth, query_step, 0)
    z_gather_wait(latents, 1)
    latent = jnp.concatenate([latents[i] for i in range(spans)], axis=1)
    pad = -latent_width % 128
    flags = jnp.where(
        (lax.broadcasted_iota(jnp.int32, (keep_count, pad), 1) == 0) & live, 1.0, 0.0
    )
    tail = jnp.concatenate([rotate(latent[:, kv_rank:], cos2, sin2), flags], axis=1)
    block = jnp.concatenate([normalized(latent[:, :kv_rank], kv_gain[...]), tail], axis=1)
    block = block.astype(BF16)
    keys[slot(c)] = block
    p_gather_start(keys, 0)
    cache_out[...] = block[:, :latent_width]
    parts = []
    for h in range(heads):
        q = query_acc[:, h * latent_width : (h + 1) * latent_width]
        parts.append(
            jnp.concatenate(
                [
                    q[:, :kv_rank],
                    rotate(q[:, kv_rank:], cos2, sin2),
                    jnp.zeros((keep_count, pad), F32),
                ],
                axis=1,
            )
        )
    query = jnp.concatenate(parts, axis=0).astype(BF16)
    tokens = n * keep_count
    rows = heads * keep_count
    key_lane = lax.broadcasted_iota(jnp.int32, (rows, tokens), 1)
    query_row = lax.broadcasted_iota(jnp.int32, (rows, tokens), 0) & (keep_count - 1)
    shift = keep_count.bit_length() - 1
    key_slot = lax.shift_right_logical(key_lane, shift)
    key_ctx = (key_slot & (half_n - 1)) * 2 + lax.shift_right_logical(
        key_slot, half_n.bit_length() - 1
    )
    causal = key_ctx * keep_count + (key_lane & (keep_count - 1)) <= query_row + c * keep_count
    pick_flag = jnp.where(
        lax.broadcasted_iota(jnp.int32, (16, latent_width + pad), 1) == latent_width, 1.0, 0.0
    ).astype(BF16)
    p_gather_forward(keys, 0)
    p_gather_finish(keys, 0)
    all_keys = keys[...].reshape(tokens, latent_width + pad)
    scores = dot_rows(query, all_keys) * SCALE
    key_live = dot_rows(pick_flag, all_keys)[:1]
    allowed = causal & (key_live > 0)
    scores = jnp.where(allowed, scores, NEGATIVE)
    highest = jnp.max(scores, axis=1, keepdims=True)
    weights = jnp.where(allowed, jnp.exp(scores - highest), 0.0)
    denominator = jnp.sum(weights, axis=1, keepdims=True)
    summed = dot(weights.astype(BF16), all_keys[:, :kv_rank]) / denominator
    mixed[slot(c)] = jnp.concatenate(
        [summed[h * keep_count : (h + 1) * keep_count] for h in range(heads)], axis=1
    ).astype(BF16)
    p_gather_start(mixed, 1)
    loads[2].wait()
    p_gather_forward(mixed, 1)
    p_gather_finish(mixed, 1)
    columns = out_w.shape[1]
    projected = dot(mixed[...].reshape(tokens, heads * kv_rank), out_w[...])
    projected = projected.reshape(n, spans, rows_dev, columns)
    for i in range(spans):
        part_send[i] = projected[:, i].reshape(n * rows_dev, columns).astype(BF16)
    z_scatter(part_send, part_recv, 2)
    attended = z_scatter_sum(part_send, part_recv, 2)
    for i in range(n):
        att_send[i] = attended[i * rows_dev : (i + 1) * rows_dev]
    for k in range(n - 1, 0, -1):
        peer = xor(c, k)
        push(
            att_send.at[slot(peer)],
            att_recv.at[c],
            "context",
            peer,
            p_send.at[2, k],
            p_recv.at[2, k],
        )
    att_recv[c] = att_send[slot(c)]
    for k in range(1, n):
        peer = xor(c, k)
        remote(
            att_send.at[slot(peer)],
            att_recv.at[peer],
            "context",
            peer,
            p_send.at[2, k],
            p_recv.at[2, k],
        ).wait_recv()
    resid = own_rows + jnp.concatenate([att_recv[i] for i in range(n)], axis=1)
    moe_in = normalized(resid, moe_gain[...])
    half_width = folded.shape[2]
    wide = jnp.concatenate(
        [moe_in, gate_lanes, jnp.zeros((rows_dev, 2 * half_width - model_width - 128), F32)],
        axis=1,
    )
    folded[s] = jnp.concatenate([wide[:, :half_width], wide[:, half_width:]], axis=0).astype(BF16)
    z_gather_start(folded, 3)
    z_gather_wait(folded, 3)
    blocks = []
    for i in range(spans):
        v = folded[i].astype(F32)
        blocks.append(
            jnp.concatenate([v[:rows_dev], v[rows_dev:]], axis=1)[:, : model_width + 128]
        )
    moe_rows[slot(c)] = jnp.concatenate(blocks, axis=0).astype(BF16)
    p_gather_start(moe_rows, 3)

    stored = (c * spans + s) // 2
    many = half_n * keep_count
    width = 512

    def expert(base, target):
        lanes = lax.broadcasted_iota(jnp.int32, (many, 128), 1)
        gate_block = moe_rows[pl.ds(base, half_n), :, model_width:].reshape(many, 128)
        scale = jnp.sum(
            jnp.where(
                (lanes == stored) | (lanes == stored + 64), gate_block.astype(F32), 0.0
            ),
            axis=1,
            keepdims=True,
        )
        gate_acc[...] = jnp.zeros_like(gate_acc)
        up_acc[...] = jnp.zeros_like(up_acc)

        def step(i, _):
            cut = pl.ds(pl.multiple_of(i * depth, depth), depth)
            x = moe_rows[pl.ds(base, half_n), :, cut].reshape(many, depth)
            gate_acc[...] += dot_rows(x, in_w[0, 0, :, cut])
            up_acc[...] += dot_rows(x, in_w[0, 1, :, cut])
            return 0

        lax.fori_loop(0, model_width // depth, step, 0)
        gate = gate_acc[...]
        hidden = (gate / (1.0 + jnp.exp(-gate)) * up_acc[...]).astype(BF16)

        def down(i, _):
            cut = pl.ds(pl.multiple_of(i * width, width), width)
            made = dot(hidden, down_w[0, :, cut]) * scale
            target[:, :, cut] = made.reshape(half_n, keep_count, width).astype(BF16)
            return 0

        lax.fori_loop(0, model_width // width, down, 0)

    p_gather_forward(moe_rows, 3)
    loads[3].wait()
    loads[4].wait()
    expert((1 - core) * half_n, pair_send)
    pair = (pair_send, pair_recv, "context", xor(c, 1), pair_sem.at[0], pair_sem.at[1])
    push(*pair)
    p_gather_finish(moe_rows, 3)
    expert(core * half_n, own_sum)
    remote(*pair).wait_recv()
    for k in range(n - 2, 0, -2):
        peer = xor(c, k)
        chip = peer // 2
        plane_send[chip] = (own_sum[chip].astype(F32) + pair_recv[chip].astype(F32)).astype(BF16)
        push(
            plane_send.at[chip],
            plane_recv.at[c // 2],
            "context",
            peer,
            p_send.at[4, k],
            p_recv.at[4, k],
        )
    total = own_sum[c // 2].astype(F32) + pair_recv[c // 2].astype(F32)
    for k in range(2, n, 2):
        peer = xor(c, k)
        chip = peer // 2
        remote(
            plane_send.at[chip],
            plane_recv.at[chip],
            "context",
            peer,
            p_send.at[4, k],
            p_recv.at[4, k],
        ).wait_recv()
        total = total + plane_recv[chip].astype(F32)
    middle = model_width // 2
    for i in range(spans):
        v = total[i * rows_dev : (i + 1) * rows_dev]
        last_send[i] = jnp.concatenate([v[:, :middle], v[:, middle:]], axis=0).astype(BF16)
    z_scatter(last_send, last_recv, 4)
    routed = z_scatter_sum(last_send, last_recv, 4)
    routed = jnp.concatenate([routed[:rows_dev], routed[rows_dev:]], axis=1)
    layer_out[...] = jnp.where(own_keep >= 0, resid + routed, 0.0).astype(BF16)
    for copy in pending:
        copy.wait_send()


def per_device(
    raw_tokens,
    keep,
    attn_gain,
    query_weight,
    latent_weight,
    kv_gain,
    out_weight,
    moe_gain,
    expert_ids,
    gate_values,
    expert_slot,
    expert_in,
    expert_out,
):
    n = lax.axis_size("context")
    spans = lax.axis_size("span")
    kv_rank = kv_gain.shape[0]
    local_latent = latent_weight.shape[1]
    latent_width = local_latent * spans
    model_width = attn_gain.shape[0]
    keep_count = keep.shape[1]
    rows_dev = expert_ids.shape[0]
    rotary_width = latent_width - kv_rank
    half = rotary_width // 2
    key_width = latent_width + (-latent_width % 128)
    many = n // 2 * keep_count
    hidden = expert_in.shape[3]
    columns = out_weight.shape[1]
    mixed_width = out_weight.shape[0]
    wide = model_width + 128
    half_width = (wide + 255) // 256 * 128
    latent_weight = latent_weight.T
    expert_in = jnp.swapaxes(expert_in, 2, 3)
    freqs = THETA ** (-2.0 * np.arange(half, dtype=np.float64) / rotary_width)
    freqs = jnp.asarray(np.tile(freqs, 2)[None, :], F32)
    vmem = pl.BlockSpec(memory_space=pltpu.VMEM)
    hbm = pl.BlockSpec(memory_space=pltpu.HBM)
    chips = n // 2
    return pl.pallas_call(
        functools.partial(kernel, n, spans),
        out_shape=(
            jax.ShapeDtypeStruct((rows_dev, model_width), BF16),
            jax.ShapeDtypeStruct((keep_count, latent_width), BF16),
        ),
        in_specs=[vmem] * 9 + [hbm] * 5,
        out_specs=(vmem, vmem),
        scratch_shapes=[
            pltpu.VMEM(query_weight.shape, BF16),
            pltpu.VMEM(latent_weight.shape, BF16),
            pltpu.VMEM(out_weight.shape, BF16),
            pltpu.VMEM(expert_in.shape, BF16),
            pltpu.VMEM(expert_out.shape, BF16),
            pltpu.VMEM((spans, keep_count, raw_tokens.shape[1]), BF16),
            pltpu.VMEM((keep_count, model_width), BF16),
            pltpu.VMEM((keep_count, query_weight.shape[1]), F32),
            pltpu.VMEM((spans, keep_count, local_latent), F32),
            pltpu.VMEM((n, keep_count, key_width), BF16),
            pltpu.VMEM((n, keep_count, mixed_width), BF16),
            pltpu.VMEM((spans, n * rows_dev, columns), BF16),
            pltpu.VMEM((spans, n * rows_dev, columns), BF16),
            pltpu.VMEM((n, rows_dev, columns), F32),
            pltpu.VMEM((n, rows_dev, columns), F32),
            pltpu.VMEM((spans, 2 * rows_dev, half_width), BF16),
            pltpu.VMEM((n, keep_count, wide), BF16),
            pltpu.VMEM((many, hidden), F32),
            pltpu.VMEM((many, hidden), F32),
            pltpu.VMEM((chips, keep_count, model_width), BF16),
            pltpu.VMEM((chips, keep_count, model_width), BF16),
            pltpu.VMEM((chips, keep_count, model_width), BF16),
            pltpu.VMEM((chips, keep_count, model_width), BF16),
            pltpu.VMEM((chips, keep_count, model_width), BF16),
            pltpu.VMEM((spans, 2 * rows_dev, model_width // 2), BF16),
            pltpu.VMEM((spans, 2 * rows_dev, model_width // 2), BF16),
            pltpu.SemaphoreType.DMA((5,)),
            pltpu.SemaphoreType.DMA((5, spans)),
            pltpu.SemaphoreType.DMA((5, spans)),
            pltpu.SemaphoreType.DMA((5, n)),
            pltpu.SemaphoreType.DMA((5, n)),
            pltpu.SemaphoreType.DMA((2,)),
        ],
        compiler_params=pltpu.CompilerParams(
            collective_id=0, has_side_effects=True, vmem_limit_bytes=53 * 1024 * 1024
        ),
    )(
        raw_tokens,
        keep,
        freqs,
        attn_gain[None, :],
        kv_gain[None, :],
        moe_gain[None, :],
        expert_ids,
        gate_values,
        expert_slot[None, :],
        query_weight,
        latent_weight,
        out_weight,
        expert_in,
        expert_out,
    )


def solution(mesh):
    placed = (
        P(("groups", "context"), "span"),
        P(("groups", "context"), None),
        P(),
        P(None, "span"),
        P(None, "span"),
        P(),
        P("span", "context"),
        P(),
        P(("groups", "context", "span"), None),
        P(("groups", "context", "span"), None),
        P(),
        P(("context", "span"), None, None, None),
        P(("context", "span"), None, None),
    )
    return jax.shard_map(
        per_device,
        mesh=mesh,
        in_specs=placed,
        out_specs=(P(("groups", "context", "span"), None), P(("groups", "context"), None)),
        check_vma=False,
    )
```

```python
import functools

import jax
import jax.numpy as jnp
import numpy as np
from jax import lax
from jax.experimental import pallas as pl
from jax.experimental.pallas import tpu as pltpu
from jax.sharding import PartitionSpec as P

EPS = 1e-06
THETA = 50000.0
SCALE = 192.0 ** (-0.5)
NEGATIVE = -1e30
F32 = jnp.float32
BF16 = jnp.bfloat16


def xor(value, bits):
    out = value
    bit = 1
    while bit <= bits:
        if bits & bit:
            out = out + bit * (1 - 2 * ((value // bit) % 2))
        bit *= 2
    return out


def rotate(values, cosine, sine):
    half = values.shape[-1] // 2
    swapped = jnp.concatenate([values[:, half:], values[:, :half]], axis=1)
    return values * cosine + swapped * sine


def normalized(values, gain):
    factor = lax.rsqrt(jnp.mean(values * values, axis=-1, keepdims=True) + EPS)
    return values * factor * gain


def dot(a, b):
    return jnp.dot(a, b, preferred_element_type=F32)


def dot_rows(a, b):
    return lax.dot_general(a, b, (((1,), (1,)), ((), ())), preferred_element_type=F32)


def column(row):
    size = row.shape[1]
    same = lax.broadcasted_iota(jnp.int32, (size, size), 0) == lax.broadcasted_iota(
        jnp.int32, (size, size), 1
    )
    return jnp.sum(jnp.where(same, row.astype(F32), 0.0), axis=1, keepdims=True).astype(jnp.int32)


def kernel(
    n,
    spans,
    raw,
    keep,
    freqs,
    attn_gain,
    kv_gain,
    moe_gain,
    ids,
    gate_values,
    slots,
    query_hbm,
    latent_hbm,
    out_hbm,
    in_hbm,
    down_hbm,
    layer_out,
    cache_out,
    query_w,
    latent_w,
    out_w,
    in_w,
    down_w,
    picked,
    normed,
    query_acc,
    latents,
    keys,
    mixed,
    part_send,
    part_recv,
    att_send,
    att_recv,
    folded,
    moe_rows,
    gate_acc,
    up_acc,
    pair_send,
    pair_recv,
    own_sum,
    plane_send,
    plane_recv,
    last_send,
    last_recv,
    load_sem,
    z_send,
    z_recv,
    p_send,
    p_recv,
    pair_sem,
):
    c = lax.axis_index("context")
    s = lax.axis_index("span")
    core = c % 2
    half_n = n // 2
    keep_count = keep.shape[1]
    rows_dev = layer_out.shape[0]
    model_width = layer_out.shape[1]
    latent_width = cache_out.shape[1]
    kv_rank = kv_gain.shape[1]
    heads = query_w.shape[1] // latent_width
    experts = slots.shape[1]
    raw_rows = raw.shape[0]

    def slot(ctx):
        return (ctx % 2) * half_n + ctx // 2

    sources = (query_hbm, latent_hbm, out_hbm, in_hbm, down_hbm)
    targets = (query_w, latent_w, out_w, in_w, down_w)
    loads = [
        pltpu.make_async_copy(a, b, load_sem.at[i])
        for i, (a, b) in enumerate(zip(sources, targets))
    ]
    for i in (1, 0, 2, 3, 4):
        loads[i].start()

    barrier = pltpu.get_barrier_semaphore()
    for k in range(1, n):
        pl.semaphore_signal(
            barrier, 1, device_id={"context": xor(c, k)}, device_id_type=pl.DeviceIdType.MESH
        )
    for k in range(1, spans):
        pl.semaphore_signal(
            barrier, 1, device_id={"span": xor(s, k)}, device_id_type=pl.DeviceIdType.MESH
        )

    def remote(src, dst, axis, peer, send, recv):
        return pltpu.make_async_remote_copy(
            src_ref=src,
            dst_ref=dst,
            send_sem=send,
            recv_sem=recv,
            device_id={axis: peer},
            device_id_type=pl.DeviceIdType.MESH,
        )

    pending = []

    def push(*args):
        copy = remote(*args)
        copy.start()
        pending.append(copy)

    def z_gather_start(buf, phase):
        for k in range(1, spans):
            push(
                buf.at[s], buf.at[s], "span", xor(s, k), z_send.at[phase, k], z_recv.at[phase, k]
            )

    def z_gather_wait(buf, phase):
        for k in range(1, spans):
            peer = xor(s, k)
            remote(
                buf.at[s], buf.at[peer], "span", peer, z_send.at[phase, k], z_recv.at[phase, k]
            ).wait_recv()

    def z_scatter(send_buf, recv_buf, phase):
        for k in range(1, spans):
            peer = xor(s, k)
            push(
                send_buf.at[peer],
                recv_buf.at[s],
                "span",
                peer,
                z_send.at[phase, k],
                z_recv.at[phase, k],
            )

    def z_scatter_sum(send_buf, recv_buf, phase):
        total = send_buf[s].astype(F32)
        for k in range(1, spans):
            peer = xor(s, k)
            remote(
                send_buf.at[peer],
                recv_buf.at[peer],
                "span",
                peer,
                z_send.at[phase, k],
                z_recv.at[phase, k],
            ).wait_recv()
            total = total + recv_buf[peer].astype(F32)
        return total

    def p_block(buf, phase, k, peer, block):
        return (
            buf.at[slot(block)],
            buf.at[slot(block)],
            "context",
            peer,
            p_send.at[phase, k],
            p_recv.at[phase, k],
        )

    def p_gather_start(buf, phase):
        for k in range(n - 1, 0, -2):
            push(*p_block(buf, phase, k, xor(c, k), c))

    def p_gather_forward(buf, phase):
        for k in range(1, n, 2):
            block = xor(c, k)
            remote(*p_block(buf, phase, k, block, block)).wait_recv()
            if k > 1:
                push(*p_block(buf, phase, k - 1, xor(c, 1), block))

    def p_gather_finish(buf, phase):
        for k in range(2, n, 2):
            block = xor(c, k)
            remote(*p_block(buf, phase, k, block, block)).wait_recv()

    listing = column(keep[...])
    live = listing >= 0
    chosen = lax.broadcasted_iota(jnp.int32, (keep_count, raw_rows), 1) == listing
    picked[s] = dot(chosen.astype(F32).astype(BF16), raw[...]).astype(BF16)

    pl.semaphore_wait(barrier, n - 1 + spans - 1)
    z_gather_start(picked, 0)
    hits = jnp.zeros((rows_dev, experts), F32)
    expert_lane = lax.broadcasted_iota(jnp.int32, (rows_dev, experts), 1)
    for t in range(ids.shape[1]):
        hits = hits + jnp.where(ids[:, t : t + 1] == expert_lane, gate_values[:, t : t + 1], 0.0)
    hits_high = hits.astype(BF16)
    hits_low = (hits - hits_high.astype(F32)).astype(BF16)
    lane = lax.broadcasted_iota(jnp.int32, (experts, 128), 1)
    slot_col = column(slots[...])
    place_high = (lane == slot_col).astype(F32).astype(BF16)
    place_low = (lane == slot_col + 64).astype(F32).astype(BF16)
    gate_lanes = dot(hits_high, place_high) + dot(hits_low, place_low)
    positions = (c * raw_rows + jnp.maximum(listing, 0)).astype(F32)
    angles = positions * freqs[...]
    cos2 = jnp.cos(angles)
    rotary = freqs.shape[1]
    first = lax.broadcasted_iota(jnp.int32, (keep_count, rotary), 1) < rotary // 2
    sin2 = jnp.where(first, -1.0, 1.0) * jnp.sin(angles)
    z_gather_wait(picked, 0)
    compact = jnp.concatenate([picked[i] for i in range(spans)], axis=1).astype(F32)
    normed[...] = normalized(compact, attn_gain[...]).astype(BF16)
    own_rows = jnp.zeros((rows_dev, model_width), F32)
    own_keep = jnp.zeros((rows_dev, 1), jnp.int32)
    for i in range(spans):
        own_rows = jnp.where(s == i, compact[i * rows_dev : (i + 1) * rows_dev], own_rows)
        own_keep = jnp.where(s == i, listing[i * rows_dev : (i + 1) * rows_dev], own_keep)

    loads[1].wait()
    latents[s] = dot_rows(normed[...], latent_w[...])
    z_gather_start(latents, 1)
    loads[0].wait()
    query_acc[...] = jnp.zeros_like(query_acc)
    depth = 512

    def query_step(i, _):
        cut = pl.ds(pl.multiple_of(i * depth, depth), depth)
        query_acc[...] += dot(normed[:, cut], query_w[cut, :])
        return 0

    lax.fori_loop(0, model_width // depth, query_step, 0)
    z_gather_wait(latents, 1)
    latent = jnp.concatenate([latents[i] for i in range(spans)], axis=1)
    pad = -latent_width % 128
    flags = jnp.where(
        (lax.broadcasted_iota(jnp.int32, (keep_count, pad), 1) == 0) & live, 1.0, 0.0
    )
    tail = jnp.concatenate([rotate(latent[:, kv_rank:], cos2, sin2), flags], axis=1)
    block = jnp.concatenate([normalized(latent[:, :kv_rank], kv_gain[...]), tail], axis=1)
    block = block.astype(BF16)
    keys[slot(c)] = block
    p_gather_start(keys, 0)
    cache_out[...] = block[:, :latent_width]
    parts = []
    for h in range(heads):
        q = query_acc[:, h * latent_width : (h + 1) * latent_width]
        parts.append(
            jnp.concatenate(
                [
                    q[:, :kv_rank],
                    rotate(q[:, kv_rank:], cos2, sin2),
                    jnp.zeros((keep_count, pad), F32),
                ],
                axis=1,
            )
        )
    query = jnp.concatenate(parts, axis=0).astype(BF16)
    tokens = n * keep_count
    rows = heads * keep_count
    key_lane = lax.broadcasted_iota(jnp.int32, (rows, tokens), 1)
    query_row = lax.broadcasted_iota(jnp.int32, (rows, tokens), 0) & (keep_count - 1)
    shift = keep_count.bit_length() - 1
    key_slot = lax.shift_right_logical(key_lane, shift)
    key_ctx = (key_slot & (half_n - 1)) * 2 + lax.shift_right_logical(
        key_slot, half_n.bit_length() - 1
    )
    causal = key_ctx * keep_count + (key_lane & (keep_count - 1)) <= query_row + c * keep_count
    pick_flag = jnp.where(
        lax.broadcasted_iota(jnp.int32, (16, latent_width + pad), 1) == latent_width, 1.0, 0.0
    ).astype(BF16)
    p_gather_forward(keys, 0)
    p_gather_finish(keys, 0)
    all_keys = keys[...].reshape(tokens, latent_width + pad)
    scores = dot_rows(query, all_keys) * SCALE
    key_live = dot_rows(pick_flag, all_keys)[:1]
    allowed = causal & (key_live > 0)
    scores = jnp.where(allowed, scores, NEGATIVE)
    highest = jnp.max(scores, axis=1, keepdims=True)
    weights = jnp.where(allowed, jnp.exp(scores - highest), 0.0)
    denominator = jnp.sum(weights, axis=1, keepdims=True)
    summed = dot(weights.astype(BF16), all_keys[:, :kv_rank]) / denominator
    mixed[slot(c)] = jnp.concatenate(
        [summed[h * keep_count : (h + 1) * keep_count] for h in range(heads)], axis=1
    ).astype(BF16)
    p_gather_start(mixed, 1)
    loads[2].wait()
    columns = out_w.shape[1]
    bases = ((1 - core) * half_n, core * half_n)
    for turn in range(2):
        if turn == 0:
            p_gather_forward(mixed, 1)
        else:
            p_gather_finish(mixed, 1)
        here = mixed[pl.ds(bases[turn], half_n)].reshape(half_n * keep_count, heads * kv_rank)
        projected = dot(here, out_w[...]).reshape(half_n, spans, rows_dev, columns)
        for i in range(spans):
            part_send[turn, i] = projected[:, i].reshape(half_n * rows_dev, columns).astype(BF16)
        z_scatter(part_send.at[turn], part_recv.at[turn], (2, 5)[turn])
    for turn in range(2):
        attended = z_scatter_sum(part_send.at[turn], part_recv.at[turn], (2, 5)[turn])
        for i in range(half_n):
            att_send[bases[turn] + i] = attended[i * rows_dev : (i + 1) * rows_dev]
        for k in range(n - 1 - turn, 0, -2):
            peer = xor(c, k)
            push(
                att_send.at[slot(peer)],
                att_recv.at[c],
                "context",
                peer,
                p_send.at[2, k],
                p_recv.at[2, k],
            )
    att_recv[c] = att_send[slot(c)]
    for k in range(1, n):
        peer = xor(c, k)
        remote(
            att_send.at[slot(peer)],
            att_recv.at[peer],
            "context",
            peer,
            p_send.at[2, k],
            p_recv.at[2, k],
        ).wait_recv()
    resid = own_rows + jnp.concatenate([att_recv[i] for i in range(n)], axis=1)
    moe_in = normalized(resid, moe_gain[...])
    half_width = folded.shape[2]
    wide = jnp.concatenate(
        [moe_in, gate_lanes, jnp.zeros((rows_dev, 2 * half_width - model_width - 128), F32)],
        axis=1,
    )
    folded[s] = jnp.concatenate([wide[:, :half_width], wide[:, half_width:]], axis=0).astype(BF16)
    z_gather_start(folded, 3)
    z_gather_wait(folded, 3)
    blocks = []
    for i in range(spans):
        v = folded[i].astype(F32)
        blocks.append(
            jnp.concatenate([v[:rows_dev], v[rows_dev:]], axis=1)[:, : model_width + 128]
        )
    moe_rows[slot(c)] = jnp.concatenate(blocks, axis=0).astype(BF16)
    p_gather_start(moe_rows, 3)

    stored = (c * spans + s) // 2
    many = half_n * keep_count
    width = 512

    def expert_up(base):
        lanes = lax.broadcasted_iota(jnp.int32, (many, 128), 1)
        gate_block = moe_rows[pl.ds(base, half_n), :, model_width:].reshape(many, 128)
        scale = jnp.sum(
            jnp.where(
                (lanes == stored) | (lanes == stored + 64), gate_block.astype(F32), 0.0
            ),
            axis=1,
            keepdims=True,
        )
        gate_acc[...] = jnp.zeros_like(gate_acc)
        up_acc[...] = jnp.zeros_like(up_acc)

        def step(i, _):
            cut = pl.ds(pl.multiple_of(i * depth, depth), depth)
            x = moe_rows[pl.ds(base, half_n), :, cut].reshape(many, depth)
            gate_acc[...] += dot_rows(x, in_w[0, 0, :, cut])
            up_acc[...] += dot_rows(x, in_w[0, 1, :, cut])
            return 0

        lax.fori_loop(0, model_width // depth, step, 0)
        gate = gate_acc[...]
        hidden = (gate / (1.0 + jnp.exp(-gate)) * up_acc[...]).astype(BF16)

        return hidden, scale

    middle = model_width // 2

    def expert_down(made_by, part, target):
        hidden, scale = made_by

        def down(i, _):
            cut = pl.ds(pl.multiple_of(i * width, width), width)
            source = pl.ds(pl.multiple_of(part * middle + i * width, width), width)
            made = dot(hidden, down_w[0, :, source]) * scale
            target[part, :, :, cut] = made.reshape(half_n, keep_count, width).astype(BF16)
            return 0

        lax.fori_loop(0, middle // width, down, 0)

    def pair(part):
        return (
            pair_send.at[part],
            pair_recv.at[part],
            "context",
            xor(c, 1),
            pair_sem.at[0, part],
            pair_sem.at[1, part],
        )

    p_gather_forward(moe_rows, 3)
    loads[3].wait()
    loads[4].wait()
    made_by = expert_up(bases[0])
    for part in range(2):
        expert_down(made_by, part, pair_send)
        push(*pair(part))
    p_gather_finish(moe_rows, 3)
    made_by = expert_up(bases[1])
    for part in range(2):
        expert_down(made_by, part, own_sum)
        remote(*pair(part)).wait_recv()
        for k in range(n - 2, 0, -2):
            peer = xor(c, k)
            chip = peer // 2
            both = own_sum[part, chip].astype(F32) + pair_recv[part, chip].astype(F32)
            plane_send[part, chip] = both.astype(BF16)
            push(
                plane_send.at[part, chip],
                plane_recv.at[part, c // 2],
                "context",
                peer,
                p_send.at[4 + part, k],
                p_recv.at[4 + part, k],
            )
    quarter = middle // 2
    for part in range(2):
        total = own_sum[part, c // 2].astype(F32) + pair_recv[part, c // 2].astype(F32)
        for k in range(2, n, 2):
            peer = xor(c, k)
            chip = peer // 2
            remote(
                plane_send.at[part, chip],
                plane_recv.at[part, chip],
                "context",
                peer,
                p_send.at[4 + part, k],
                p_recv.at[4 + part, k],
            ).wait_recv()
            total = total + plane_recv[part, chip].astype(F32)
        for i in range(spans):
            v = total[i * rows_dev : (i + 1) * rows_dev]
            last_send[part, i] = jnp.concatenate([v[:, :quarter], v[:, quarter:]], axis=0).astype(
                BF16
            )
        z_scatter(last_send.at[part], last_recv.at[part], (4, 6)[part])
    pieces = []
    for part in range(2):
        v = z_scatter_sum(last_send.at[part], last_recv.at[part], (4, 6)[part])
        pieces += [v[:rows_dev], v[rows_dev:]]
    routed = jnp.concatenate(pieces, axis=1)
    layer_out[...] = jnp.where(own_keep >= 0, resid + routed, 0.0).astype(BF16)
    for copy in pending:
        copy.wait_send()


def per_device(
    raw_tokens,
    keep,
    attn_gain,
    query_weight,
    latent_weight,
    kv_gain,
    out_weight,
    moe_gain,
    expert_ids,
    gate_values,
    expert_slot,
    expert_in,
    expert_out,
):
    n = lax.axis_size("context")
    spans = lax.axis_size("span")
    kv_rank = kv_gain.shape[0]
    local_latent = latent_weight.shape[1]
    latent_width = local_latent * spans
    model_width = attn_gain.shape[0]
    keep_count = keep.shape[1]
    rows_dev = expert_ids.shape[0]
    rotary_width = latent_width - kv_rank
    half = rotary_width // 2
    key_width = latent_width + (-latent_width % 128)
    many = n // 2 * keep_count
    hidden = expert_in.shape[3]
    columns = out_weight.shape[1]
    mixed_width = out_weight.shape[0]
    wide = model_width + 128
    half_width = (wide + 255) // 256 * 128
    latent_weight = latent_weight.T
    expert_in = jnp.swapaxes(expert_in, 2, 3)
    freqs = THETA ** (-2.0 * np.arange(half, dtype=np.float64) / rotary_width)
    freqs = jnp.asarray(np.tile(freqs, 2)[None, :], F32)
    vmem = pl.BlockSpec(memory_space=pltpu.VMEM)
    hbm = pl.BlockSpec(memory_space=pltpu.HBM)
    chips = n // 2
    return pl.pallas_call(
        functools.partial(kernel, n, spans),
        out_shape=(
            jax.ShapeDtypeStruct((rows_dev, model_width), BF16),
            jax.ShapeDtypeStruct((keep_count, latent_width), BF16),
        ),
        in_specs=[vmem] * 9 + [hbm] * 5,
        out_specs=(vmem, vmem),
        scratch_shapes=[
            pltpu.VMEM(query_weight.shape, BF16),
            pltpu.VMEM(latent_weight.shape, BF16),
            pltpu.VMEM(out_weight.shape, BF16),
            pltpu.VMEM(expert_in.shape, BF16),
            pltpu.VMEM(expert_out.shape, BF16),
            pltpu.VMEM((spans, keep_count, raw_tokens.shape[1]), BF16),
            pltpu.VMEM((keep_count, model_width), BF16),
            pltpu.VMEM((keep_count, query_weight.shape[1]), F32),
            pltpu.VMEM((spans, keep_count, local_latent), F32),
            pltpu.VMEM((n, keep_count, key_width), BF16),
            pltpu.VMEM((n, keep_count, mixed_width), BF16),
            pltpu.VMEM((2, spans, chips * rows_dev, columns), BF16),
            pltpu.VMEM((2, spans, chips * rows_dev, columns), BF16),
            pltpu.VMEM((n, rows_dev, columns), F32),
            pltpu.VMEM((n, rows_dev, columns), F32),
            pltpu.VMEM((spans, 2 * rows_dev, half_width), BF16),
            pltpu.VMEM((n, keep_count, wide), BF16),
            pltpu.VMEM((many, hidden), F32),
            pltpu.VMEM((many, hidden), F32),
            pltpu.VMEM((2, chips, keep_count, model_width // 2), BF16),
            pltpu.VMEM((2, chips, keep_count, model_width // 2), BF16),
            pltpu.VMEM((2, chips, keep_count, model_width // 2), BF16),
            pltpu.VMEM((2, chips, keep_count, model_width // 2), BF16),
            pltpu.VMEM((2, chips, keep_count, model_width // 2), BF16),
            pltpu.VMEM((2, spans, 2 * rows_dev, model_width // 4), BF16),
            pltpu.VMEM((2, spans, 2 * rows_dev, model_width // 4), BF16),
            pltpu.SemaphoreType.DMA((5,)),
            pltpu.SemaphoreType.DMA((7, spans)),
            pltpu.SemaphoreType.DMA((7, spans)),
            pltpu.SemaphoreType.DMA((6, n)),
            pltpu.SemaphoreType.DMA((6, n)),
            pltpu.SemaphoreType.DMA((2, 2)),
        ],
        compiler_params=pltpu.CompilerParams(
            collective_id=0, has_side_effects=True, vmem_limit_bytes=56 * 1024 * 1024
        ),
    )(
        raw_tokens,
        keep,
        freqs,
        attn_gain[None, :],
        kv_gain[None, :],
        moe_gain[None, :],
        expert_ids,
        gate_values,
        expert_slot[None, :],
        query_weight,
        latent_weight,
        out_weight,
        expert_in,
        expert_out,
    )


def solution(mesh):
    placed = (
        P(("groups", "context"), "span"),
        P(("groups", "context"), None),
        P(),
        P(None, "span"),
        P(None, "span"),
        P(),
        P("span", "context"),
        P(),
        P(("groups", "context", "span"), None),
        P(("groups", "context", "span"), None),
        P(),
        P(("context", "span"), None, None, None),
        P(("context", "span"), None, None),
    )
    return jax.shard_map(
        per_device,
        mesh=mesh,
        in_specs=placed,
        out_specs=(P(("groups", "context", "span"), None), P(("groups", "context"), None)),
        check_vma=False,
    )
```
